32 devices in a mesh: parts: 2 (over y), tm: 8 (over z, x), chan: 2 (over core).
Axes of the slice: x: 2, y: 2, z: 4, core: 2. Of those that a mesh axis runs over, the one named last changes fastest.
Arguments:
- signal: bfloat16 [16384, 1024], P(('parts', 'tm'), 'chan'), parts along dimension 0, may hold values from -6 to 6
- kernel_weight_stack: bfloat16 [2, 16, 128, 128], P(None, 'chan'), may hold values from -0.5 to 0.5
- conv_bias: float32 [2, 16, 128], P(None, 'chan'), may hold values from -4 to 4
- mix_weight: bfloat16 [2, 1024, 1024], P(None, None, 'chan'), may hold values from -0.1875 to 0.1875
Outputs:
- output: bfloat16 [16384, 1024], P(('parts', 'tm'), 'chan'), parts along dimension 0
The draws below stay inside these ranges and needn't reach their ends.
There are 2 independent parts, one for each index of `parts`. The reference program is written for one: setup_inputs(seed, part) draws one part's arguments, and reference() takes and returns one part's arrays. A program takes and returns all parts, laid end to end along the dimension named above; an argument that names none is the same for every part. Nothing has to cross between parts.
All inputs are finite; a program needn't handle non-finite values.
Results may differ from the reference program's by a relative error of at most 0.0049.
The reference program's roundings to bfloat16 on the way count: a program that leaves them out, or rounds other values in their place, can miss the bound.
Values may be sent and summed in bfloat16 or wider, within the bound.
A program may use at most 64 MiB of HBM per device.

```python
import jax
import jax.numpy as jnp
from jax import lax

C = 1024
G = 16
CG = 64
SECOND_DILATION = 4096
LAYERS = 2
ROUNDS = 8192


def shard_levels(own_key, extent, shards, smallest, high):
    factor_of = 1.0
    for axis_at, shards_of in shards:
        steps = jax.random.uniform(jax.random.fold_in(jax.random.fold_in(own_key, 6), axis_at), (shards_of,), jnp.float32, smallest / len(shards), high / len(shards))
        factor_of = factor_of * jnp.repeat(jnp.exp(steps), extent[axis_at] // shards_of).reshape((-1,) + (1,) * (len(extent) - 1 - axis_at))
    return factor_of


def centred(rng, extent, width, bound, split=(), dtype=jnp.bfloat16):
    loudness = shard_levels(rng, extent, split, -0.22, 0.18) if split else 1.0
    entries = jax.random.normal(rng, extent, jnp.float32) * width * loudness
    return jnp.minimum(jnp.maximum(entries, -bound), bound).astype(dtype)


def setup_inputs(seed: int = 0, part: int = 0) -> dict:
    seeds = jax.random.split(jax.random.key(seed), 5)
    part_splits = jax.random.split(jax.random.fold_in(seeds[4], part), 5)
    return {
        "signal": centred(part_splits[0], (ROUNDS, C), 1.0, 6.0, ((0, 8), (1, 2))),
        "kernel_weight_stack": centred(seeds[1], (LAYERS, G, 2 * CG, 2 * CG), (2 * CG) ** -0.5, 0.5, ((1, 2),)),
        "conv_bias": centred(seeds[2], (LAYERS, G, 2 * CG), 1.0, 4.0, ((1, 2),), jnp.float32),
        "mix_weight": centred(seeds[3], (LAYERS, C, C), C ** -0.5, 0.1875, ((2, 2),)),
    }


def reference(signal, kernel_weight_stack, conv_bias, mix_weight):
    current = signal
    for layer_position_index, dilation_rounds in enumerate((1, SECOND_DILATION)):
        earlier = jnp.concatenate([jnp.zeros((dilation_rounds, C), jnp.bfloat16), current[:-dilation_rounds]], axis=0)
        stacked = jnp.concatenate([earlier.reshape(ROUNDS, G, CG), current.reshape(ROUNDS, G, CG)], axis=2).astype(jnp.float32)
        mixed = jnp.einsum("rgk,gkn->rgn", stacked, kernel_weight_stack[layer_position_index].astype(jnp.float32), precision=lax.Precision.HIGHEST)
        mixed = mixed + conv_bias[layer_position_index][None, :, :]
        hidden = jnp.tanh(mixed[:, :, :CG]) * jax.nn.sigmoid(mixed[:, :, CG:])
        hidden = hidden.reshape(ROUNDS, C).astype(jnp.bfloat16)
        mixing = jnp.dot(hidden.astype(jnp.float32), mix_weight[layer_position_index].astype(jnp.float32), precision=lax.Precision.HIGHEST)
        current = (current.astype(jnp.float32) + mixing).astype(jnp.bfloat16)
    return current
```

```python
import functools

import jax
import jax.numpy as jnp
from jax import lax
from jax.experimental import pallas as pl
from jax.experimental.pallas import tpu as pltpu
from jax.sharding import PartitionSpec as P

SECOND_DILATION = 4096
EDGE = 16
MESH = pl.DeviceIdType.MESH


def layers_kernel(
    length, reach, rows, raw_rows,
    sig, kws, bias, mix, out,
    xbuf, raw, far, x1, hid, oth, kv, wp, bv, bp, mv, obuf,
    load_sem, edge_sem, raw_sem, fwd_sem, x1_send, x1_recv, hid_send, hid_recv, out_sem,
):
    total, width = sig.shape
    groups, taps = kws.shape[1], kws.shape[2]
    half = taps // 2
    pairs = groups // 2
    chunks, raw_chunks = total // rows, raw_rows // rows
    part, t, c = lax.axis_index("parts"), lax.axis_index("tm"), lax.axis_index("chan")
    has_next, has_prev = t < length - 1, t > 0
    sends, receives = t < length - reach, t >= reach

    def at(step):
        return (part, lax.rem(t + step + length, length), c)

    peer = (part, t, 1 - c)

    barrier = pltpu.get_barrier_semaphore()
    for there, step in ((has_next, 1), (has_prev, -1), (sends, reach), (receives, -reach)):

        @pl.when(there)
        def _(step=step):
            pl.semaphore_signal(barrier, inc=1, device_id=at(step), device_id_type=MESH)

    pl.semaphore_signal(barrier, inc=1, device_id=peer, device_id_type=MESH)

    loads = [
        pltpu.make_async_copy(src, dst, load_sem.at[i])
        for i, (src, dst) in enumerate(
            (
                (kws, kv),
                (bias, bv),
                (sig, xbuf.at[pl.ds(EDGE, total)]),
                (mix.at[0], mv.at[0]),
                (mix.at[1], mv.at[1]),
            )
        )
    ]
    for copy in loads:
        copy.start()

    partners = 1
    for there in (has_next, has_prev, sends, receives):
        partners = partners + there.astype(jnp.int32)
    pl.semaphore_wait(barrier, partners)

    def remote(src, dst, send, recv, to):
        return pltpu.make_async_remote_copy(
            src_ref=src, dst_ref=dst, send_sem=send, recv_sem=recv, device_id=to, device_id_type=MESH
        )

    edge_copy = remote(
        sig.at[pl.ds(total - EDGE, EDGE)], xbuf.at[pl.ds(0, EDGE)], edge_sem.at[0], edge_sem.at[1], at(1)
    )
    raw_copy = remote(
        sig.at[pl.ds(0, raw_rows)], raw.at[pl.ds(EDGE, raw_rows)], raw_sem.at[0], raw_sem.at[1], at(reach)
    )
    raw_edge_copy = remote(
        xbuf.at[pl.ds(0, EDGE)], raw.at[pl.ds(0, EDGE)], fwd_sem.at[0], fwd_sem.at[1], at(reach)
    )
    pl.when(has_next)(edge_copy.start)
    pl.when(sends)(raw_copy.start)

    def block(k, offset=0, size=rows):
        return pl.ds(pl.multiple_of(k * rows + offset, EDGE), size)

    def x1_copy(k):
        return remote(x1.at[block(k)], far.at[block(k)], x1_send.at[k], x1_recv.at[k], at(reach))

    def hid_copy(k):
        return remote(hid.at[block(k)], oth.at[block(k)], hid_send.at[k], hid_recv.at[k], peer)

    def out_copy(k):
        return pltpu.make_async_copy(obuf.at[block(k)], out.at[block(k)], out_sem.at[k])

    def pack_weights(layer):
        zero = jnp.zeros((half, half), jnp.bfloat16)
        for p in range(pairs):
            even, odd = kv[layer, 2 * p], kv[layer, 2 * p + 1]
            for tap in range(2):
                e, o = even[tap * half : (tap + 1) * half], odd[tap * half : (tap + 1) * half]
                top, low = tap * taps, tap * taps + half
                wp[layer, p, top : top + half, :] = jnp.concatenate(
                    [e[:, :half], zero, e[:, half:], zero], axis=1
                )
                wp[layer, p, low : low + half, :] = jnp.concatenate(
                    [zero, o[:, :half], zero, o[:, half:]], axis=1
                )
            be, bo = bv[layer, 2 * p : 2 * p + 1], bv[layer, 2 * p + 1 : 2 * p + 2]
            at_row = layer * pairs + p
            bp[at_row : at_row + 1, :] = jnp.concatenate(
                [be[:, :half], bo[:, :half], be[:, half:], bo[:, half:]], axis=1
            )

    def gated(slot, layer, earlier, current):
        for p in range(pairs):
            cols = slice(p * taps, (p + 1) * taps)
            z = jnp.dot(
                jnp.concatenate([earlier[:, cols], current[:, cols]], axis=1),
                wp[layer, p],
                preferred_element_type=jnp.float32,
            )
            row = layer * pairs + p
            z = z + bp[row : row + 1, :]
            h = jnp.tanh(z[:, :taps]) * (0.5 * jnp.tanh(0.5 * z[:, taps:]) + 0.5)
            hid[block(slot), cols] = h.astype(jnp.bfloat16)
        hid_copy(slot).start()

    def mixed(slot, layer, current):
        mine = mv[layer, pl.ds(pl.multiple_of(c * width, width), width), :]
        theirs = mv[layer, pl.ds(pl.multiple_of((1 - c) * width, width), width), :]
        acc = jnp.dot(hid[block(slot)], mine, preferred_element_type=jnp.float32)
        hid_copy(slot).wait_recv()
        acc = acc + jnp.dot(oth[block(slot)], theirs, preferred_element_type=jnp.float32)
        return (current.astype(jnp.float32) + acc).astype(jnp.bfloat16)

    def first_gated(buf, k, slot):
        window = buf[block(k, size=rows + EDGE)]
        shifted = pltpu.roll(window.astype(jnp.float32), 1, 0)[EDGE:].astype(jnp.bfloat16)
        gated(slot, 0, shifted, window[EDGE:])

    def own_finish(k):
        x1[block(k)] = mixed(k, 0, xbuf[block(k, EDGE)])

        @pl.when(jnp.logical_and(sends, k >= raw_chunks))
        def _():
            x1_copy(k).start()

    loads[0].wait()
    loads[1].wait()
    pack_weights(0)

    @pl.when(jnp.logical_not(has_prev))
    def _():
        xbuf[:EDGE] = jnp.zeros((EDGE, width), jnp.bfloat16)

    @pl.when(jnp.logical_not(receives))
    def _():
        far[...] = jnp.zeros((total, width), jnp.bfloat16)

    pl.when(has_prev)(edge_copy.wait_recv)
    pl.when(sends)(raw_edge_copy.start)
    loads[2].wait()
    first_gated(xbuf, 0, 0)
    loads[3].wait()

    @pl.loop(1, chunks)
    def _(k):
        first_gated(xbuf, k, k)
        own_finish(k - 1)

    own_finish(chunks - 1)

    pack_weights(1)
    loads[4].wait()

    @pl.when(receives)
    def _():
        raw_copy.wait_recv()
        raw_edge_copy.wait_recv()

        @pl.loop(0, raw_chunks)
        def _(k):
            first_gated(raw, k, chunks + k)
            far[block(k)] = mixed(chunks + k, 0, raw[block(k, EDGE)])

    @pl.loop(0, chunks)
    def _(k):
        @pl.when(jnp.logical_and(receives, k >= raw_chunks))
        def _():
            x1_copy(k).wait_recv()

        slot = chunks + raw_chunks + k
        current = x1[block(k)]
        gated(slot, 1, far[block(k)], current)
        obuf[block(k)] = mixed(slot, 1, current)
        out_copy(k).start()

    @pl.loop(0, chunks)
    def _(k):
        out_copy(k).wait()
        hid_copy(k).wait_send()
        hid_copy(chunks + raw_chunks + k).wait_send()

        @pl.when(jnp.logical_and(sends, k >= raw_chunks))
        def _():
            x1_copy(k).wait_send()

    @pl.when(receives)
    def _():
        @pl.loop(0, raw_chunks)
        def _(k):
            hid_copy(chunks + k).wait_send()

    pl.when(has_next)(edge_copy.wait_send)

    @pl.when(sends)
    def _():
        raw_copy.wait_send()
        raw_edge_copy.wait_send()


def shards(length, signal, kernel_weight_stack, conv_bias, mix_weight):
    total, width = signal.shape
    layers, groups, taps, _ = kernel_weight_stack.shape
    reach = SECOND_DILATION // total
    rows, raw_rows = 64, 128
    chunks = total // rows
    slots = 2 * chunks + raw_rows // rows
    bf16, f32 = jnp.bfloat16, jnp.float32
    dma = pltpu.SemaphoreType.DMA
    return pl.pallas_call(
        functools.partial(layers_kernel, length, reach, rows, raw_rows),
        out_shape=jax.ShapeDtypeStruct(signal.shape, bf16),
        in_specs=[pl.BlockSpec(memory_space=pltpu.HBM)] * 4,
        out_specs=pl.BlockSpec(memory_space=pl.ANY),
        scratch_shapes=[
            pltpu.VMEM((EDGE + total, width), bf16),
            pltpu.VMEM((EDGE + raw_rows, width), bf16),
            pltpu.VMEM((total, width), bf16),
            pltpu.VMEM((total, width), bf16),
            pltpu.VMEM((slots * rows, width), bf16),
            pltpu.VMEM((slots * rows, width), bf16),
            pltpu.VMEM(kernel_weight_stack.shape, bf16),
            pltpu.VMEM((layers, groups // 2, 2 * taps, 2 * taps), bf16),
            pltpu.VMEM(conv_bias.shape, f32),
            pltpu.VMEM((layers * groups // 2, 2 * taps), f32),
            pltpu.VMEM(mix_weight.shape, bf16),
            pltpu.VMEM((total, width), bf16),
            dma((5,)),
            dma((2,)),
            dma((2,)),
            dma((2,)),
            dma((chunks,)),
            dma((chunks,)),
            dma((slots,)),
            dma((slots,)),
            dma((chunks,)),
        ],
        compiler_params=pltpu.CompilerParams(
            collective_id=0, has_side_effects=True, vmem_limit_bytes=40 << 20
        ),
    )(signal, kernel_weight_stack, conv_bias, mix_weight)


def solution(mesh):
    placed = (
        P(("parts", "tm"), "chan"),
        P(None, "chan", None, None),
        P(None, "chan", None),
        P(None, None, "chan"),
    )
    return jax.shard_map(
        functools.partial(shards, mesh.shape["tm"]),
        mesh=mesh,
        in_specs=placed,
        out_specs=P(("parts", "tm"), "chan"),
        check_vma=False,
    )
```

```python
import functools

import jax
import jax.numpy as jnp
from jax import lax
from jax.experimental import pallas as pl
from jax.experimental.pallas import tpu as pltpu
from jax.sharding import PartitionSpec as P

SECOND_DILATION = 4096
EDGE = 16
MESH = pl.DeviceIdType.MESH


def layers_kernel(
    length, reach, rows, raw_rows,
    sig, kws, bias, mix, out,
    xbuf, raw, far, x1, hid, oth, kv, wp, bv, bp, mv, obuf,
    load_sem, edge_sem, raw_sem, fwd_sem, x1_send, x1_recv, hid_send, hid_recv, out_sem,
):
    total, width = sig.shape
    groups, taps = kws.shape[1], kws.shape[2]
    half = taps // 2
    pairs = groups // 2
    chunks, raw_chunks = total // rows, raw_rows // rows
    part, t, c = lax.axis_index("parts"), lax.axis_index("tm"), lax.axis_index("chan")
    has_next, has_prev = t < length - 1, t > 0
    sends, receives = t < length - reach, t >= reach

    def at(step):
        return (part, lax.rem(t + step + length, length), c)

    peer = (part, t, 1 - c)

    barrier = pltpu.get_barrier_semaphore()
    for there, step in ((has_next, 1), (has_prev, -1), (sends, reach), (receives, -reach)):

        @pl.when(there)
        def _(step=step):
            pl.semaphore_signal(barrier, inc=1, device_id=at(step), device_id_type=MESH)

    pl.semaphore_signal(barrier, inc=1, device_id=peer, device_id_type=MESH)

    loads = [
        pltpu.make_async_copy(src, dst, load_sem.at[i])
        for i, (src, dst) in enumerate(
            (
                (kws, kv),
                (bias, bv),
                (sig, xbuf.at[pl.ds(EDGE, total)]),
                (mix.at[0], mv.at[0]),
                (mix.at[1], mv.at[1]),
            )
        )
    ]
    for copy in loads:
        copy.start()

    partners = 1
    for there in (has_next, has_prev, sends, receives):
        partners = partners + there.astype(jnp.int32)
    pl.semaphore_wait(barrier, partners)

    def remote(src, dst, send, recv, to):
        return pltpu.make_async_remote_copy(
            src_ref=src, dst_ref=dst, send_sem=send, recv_sem=recv, device_id=to, device_id_type=MESH
        )

    edge_copy = remote(
        sig.at[pl.ds(total - EDGE, EDGE)], xbuf.at[pl.ds(0, EDGE)], edge_sem.at[0], edge_sem.at[1], at(1)
    )
    raw_copy = remote(
        sig.at[pl.ds(0, raw_rows)], raw.at[pl.ds(EDGE, raw_rows)], raw_sem.at[0], raw_sem.at[1], at(reach)
    )
    raw_edge_copy = remote(
        xbuf.at[pl.ds(0, EDGE)], raw.at[pl.ds(0, EDGE)], fwd_sem.at[0], fwd_sem.at[1], at(reach)
    )
    pl.when(has_next)(edge_copy.start)
    pl.when(sends)(raw_copy.start)

    def block(k, offset=0, size=rows):
        return pl.ds(pl.multiple_of(k * rows + offset, EDGE), size)

    def x1_copy(k):
        return remote(x1.at[block(k)], far.at[block(k)], x1_send.at[k], x1_recv.at[k], at(reach))

    def hid_copy(k):
        return remote(hid.at[block(k)], oth.at[block(k)], hid_send.at[k], hid_recv.at[k], peer)

    def out_copy(k):
        return pltpu.make_async_copy(obuf.at[block(k)], out.at[block(k)], out_sem.at[k])

    def pack_weights(layer):
        zero = jnp.zeros((half, half), jnp.bfloat16)
        for p in range(pairs):
            even, odd = kv[layer, 2 * p], kv[layer, 2 * p + 1]
            for tap in range(2):
                e, o = even[tap * half : (tap + 1) * half], odd[tap * half : (tap + 1) * half]
                top, low = tap * taps, tap * taps + half
                wp[layer, p, top : top + half, :] = jnp.concatenate(
                    [e[:, :half], zero, e[:, half:], zero], axis=1
                )
                wp[layer, p, low : low + half, :] = jnp.concatenate(
                    [zero, o[:, :half], zero, o[:, half:]], axis=1
                )
            be, bo = bv[layer, 2 * p : 2 * p + 1], bv[layer, 2 * p + 1 : 2 * p + 2]
            at_row = layer * pairs + p
            bp[at_row : at_row + 1, :] = jnp.concatenate(
                [be[:, :half], bo[:, :half], be[:, half:], bo[:, half:]], axis=1
            )

    def gated(slot, layer, earlier, current):
        for p in range(pairs):
            cols = slice(p * taps, (p + 1) * taps)
            z = jnp.dot(
                jnp.concatenate([earlier[:, cols], current[:, cols]], axis=1),
                wp[layer, p],
                preferred_element_type=jnp.float32,
            )
            row = layer * pairs + p
            z = z + bp[row : row + 1, :]
            h = jnp.tanh(z[:, :taps]) * (0.5 * jnp.tanh(0.5 * z[:, taps:]) + 0.5)
            hid[block(slot), cols] = h.astype(jnp.bfloat16)
        hid_copy(slot).start()

    def mixed(slot, layer, current):
        mine = mv[layer, pl.ds(pl.multiple_of(c * width, width), width), :]
        theirs = mv[layer, pl.ds(pl.multiple_of((1 - c) * width, width), width), :]
        acc = jnp.dot(hid[block(slot)], mine, preferred_element_type=jnp.float32)
        hid_copy(slot).wait_recv()
        acc = acc + jnp.dot(oth[block(slot)], theirs, preferred_element_type=jnp.float32)
        return (current.astype(jnp.float32) + acc).astype(jnp.bfloat16)

    def first_gated(buf, k, slot):
        window = buf[block(k, size=rows + EDGE)]
        shifted = pltpu.roll(window.astype(jnp.float32), 1, 0)[EDGE:].astype(jnp.bfloat16)
        gated(slot, 0, shifted, window[EDGE:])

    def own_finish(k):
        x1[block(k)] = mixed(k, 0, xbuf[block(k, EDGE)])

        @pl.when(jnp.logical_and(sends, k >= raw_chunks))
        def _():
            x1_copy(k).start()

    loads[0].wait()
    loads[1].wait()
    pack_weights(0)

    @pl.when(jnp.logical_not(has_prev))
    def _():
        xbuf[:EDGE] = jnp.zeros((EDGE, width), jnp.bfloat16)

    @pl.when(jnp.logical_not(receives))
    def _():
        far[...] = jnp.zeros((total, width), jnp.bfloat16)

    pl.when(has_prev)(edge_copy.wait_recv)
    pl.when(sends)(raw_edge_copy.start)
    loads[2].wait()
    first_gated(xbuf, 0, 0)
    loads[3].wait()

    @pl.loop(1, chunks)
    def _(k):
        first_gated(xbuf, k, k)
        own_finish(k - 1)

    own_finish(chunks - 1)

    pack_weights(1)
    loads[4].wait()

    @pl.when(receives)
    def _():
        raw_copy.wait_recv()
        raw_edge_copy.wait_recv()

        @pl.loop(0, raw_chunks)
        def _(k):
            first_gated(raw, k, chunks + k)
            far[block(k)] = mixed(chunks + k, 0, raw[block(k, EDGE)])

    @pl.loop(0, chunks)
    def _(k):
        @pl.when(jnp.logical_and(receives, k >= raw_chunks))
        def _():
            x1_copy(k).wait_recv()

        slot = chunks + raw_chunks + k
        current = x1[block(k)]
        gated(slot, 1, far[block(k)], current)
        obuf[block(k)] = mixed(slot, 1, current)
        out_copy(k).start()

    @pl.loop(0, chunks)
    def _(k):
        out_copy(k).wait()
        hid_copy(k).wait_send()
        hid_copy(chunks + raw_chunks + k).wait_send()

        @pl.when(jnp.logical_and(sends, k >= raw_chunks))
        def _():
            x1_copy(k).wait_send()

    @pl.when(receives)
    def _():
        @pl.loop(0, raw_chunks)
        def _(k):
            hid_copy(chunks + k).wait_send()

    pl.when(has_next)(edge_copy.wait_send)

    @pl.when(sends)
    def _():
        raw_copy.wait_send()
        raw_edge_copy.wait_send()


def shards(length, signal, kernel_weight_stack, conv_bias, mix_weight):
    total, width = signal.shape
    layers, groups, taps, _ = kernel_weight_stack.shape
    reach = SECOND_DILATION // total
    rows, raw_rows = 128, 128
    chunks = total // rows
    slots = 2 * chunks + raw_rows // rows
    bf16, f32 = jnp.bfloat16, jnp.float32
    dma = pltpu.SemaphoreType.DMA
    return pl.pallas_call(
        functools.partial(layers_kernel, length, reach, rows, raw_rows),
        out_shape=jax.ShapeDtypeStruct(signal.shape, bf16),
        in_specs=[pl.BlockSpec(memory_space=pltpu.HBM)] * 4,
        out_specs=pl.BlockSpec(memory_space=pl.ANY),
        scratch_shapes=[
            pltpu.VMEM((EDGE + total, width), bf16),
            pltpu.VMEM((EDGE + raw_rows, width), bf16),
            pltpu.VMEM((total, width), bf16),
            pltpu.VMEM((total, width), bf16),
            pltpu.VMEM((slots * rows, width), bf16),
            pltpu.VMEM((slots * rows, width), bf16),
            pltpu.VMEM(kernel_weight_stack.shape, bf16),
            pltpu.VMEM((layers, groups // 2, 2 * taps, 2 * taps), bf16),
            pltpu.VMEM(conv_bias.shape, f32),
            pltpu.VMEM((layers * groups // 2, 2 * taps), f32),
            pltpu.VMEM(mix_weight.shape, bf16),
            pltpu.VMEM((total, width), bf16),
            dma((5,)),
            dma((2,)),
            dma((2,)),
            dma((2,)),
            dma((chunks,)),
            dma((chunks,)),
            dma((slots,)),
            dma((slots,)),
            dma((chunks,)),
        ],
        compiler_params=pltpu.CompilerParams(
            collective_id=0, has_side_effects=True, vmem_limit_bytes=40 << 20
        ),
    )(signal, kernel_weight_stack, conv_bias, mix_weight)


def solution(mesh):
    placed = (
        P(("parts", "tm"), "chan"),
        P(None, "chan", None, None),
        P(None, "chan", None),
        P(None, None, "chan"),
    )
    return jax.shard_map(
        functools.partial(shards, mesh.shape["tm"]),
        mesh=mesh,
        in_specs=placed,
        out_specs=P(("parts", "tm"), "chan"),
        check_vma=False,
    )
```

```python
import functools

import jax
import jax.numpy as jnp
from jax import lax
from jax.experimental import pallas as pl
from jax.experimental.pallas import tpu as pltpu
from jax.sharding import PartitionSpec as P

SECOND_DILATION = 4096
EDGE = 16
MESH = pl.DeviceIdType.MESH


def layers_kernel(
    length, reach, rows, raw_rows,
    sig, kws, bias, mix, out,
    xbuf, raw, far, x1, hid, oth, kv, wp, bv, bp, mv, obuf,
    load_sem, edge_sem, raw_sem, fwd_sem, x1_send, x1_recv, hid_send, hid_recv, out_sem,
):
    total, width = sig.shape
    groups, taps = kws.shape[1], kws.shape[2]
    half = taps // 2
    pairs = groups // 2
    chunks, raw_chunks = total // rows, raw_rows // rows
    part, t, c = lax.axis_index("parts"), lax.axis_index("tm"), lax.axis_index("chan")
    has_next, has_prev = t < length - 1, t > 0
    sends, receives = t < length - reach, t >= reach

    def at(step):
        return (part, lax.rem(t + step + length, length), c)

    peer = (part, t, 1 - c)

    barrier = pltpu.get_barrier_semaphore()
    for there, step in ((has_next, 1), (has_prev, -1), (sends, reach), (receives, -reach)):

        @pl.when(there)
        def _(step=step):
            pl.semaphore_signal(barrier, inc=1, device_id=at(step), device_id_type=MESH)

    pl.semaphore_signal(barrier, inc=1, device_id=peer, device_id_type=MESH)

    loads = [
        pltpu.make_async_copy(src, dst, load_sem.at[i])
        for i, (src, dst) in enumerate(
            (
                (kws, kv),
                (bias, bv),
                (sig.at[pl.ds(raw_rows, total - raw_rows)], xbuf.at[pl.ds(EDGE + raw_rows, total - raw_rows)]),
                (mix.at[0], mv.at[0]),
                (mix.at[1], mv.at[1]),
            )
        )
    ]
    head_copy = pltpu.make_async_copy(
        sig.at[pl.ds(0, raw_rows)], xbuf.at[pl.ds(EDGE, raw_rows)], load_sem.at[5]
    )
    head_copy.start()
    for i in (2, 0, 1, 3, 4):
        loads[i].start()

    partners = 1
    for there in (has_next, has_prev, sends, receives):
        partners = partners + there.astype(jnp.int32)
    pl.semaphore_wait(barrier, partners)

    def remote(src, dst, send, recv, to):
        return pltpu.make_async_remote_copy(
            src_ref=src, dst_ref=dst, send_sem=send, recv_sem=recv, device_id=to, device_id_type=MESH
        )

    edge_copy = remote(
        xbuf.at[pl.ds(total, EDGE)], xbuf.at[pl.ds(0, EDGE)], edge_sem.at[0], edge_sem.at[1], at(1)
    )
    raw_copy = remote(
        xbuf.at[pl.ds(EDGE, raw_rows)], raw.at[pl.ds(EDGE, raw_rows)], raw_sem.at[0], raw_sem.at[1], at(reach)
    )
    raw_edge_copy = remote(
        xbuf.at[pl.ds(0, EDGE)], raw.at[pl.ds(0, EDGE)], fwd_sem.at[0], fwd_sem.at[1], at(reach)
    )
    head_copy.wait()
    pl.when(sends)(raw_copy.start)
    loads[2].wait()
    pl.when(has_next)(edge_copy.start)

    def block(k, offset=0, size=rows):
        return pl.ds(pl.multiple_of(k * rows + offset, EDGE), size)

    def x1_copy(k):
        return remote(x1.at[block(k)], far.at[block(k)], x1_send.at[k], x1_recv.at[k], at(reach))

    def hid_copy(k):
        return remote(hid.at[block(k)], oth.at[block(k)], hid_send.at[k], hid_recv.at[k], peer)

    def out_copy(k):
        return pltpu.make_async_copy(obuf.at[block(k)], out.at[block(k)], out_sem.at[k])

    def pack_weights(layer):
        zero = jnp.zeros((half, half), jnp.bfloat16)
        for p in range(pairs):
            even, odd = kv[layer, 2 * p], kv[layer, 2 * p + 1]
            for tap in range(2):
                e, o = even[tap * half : (tap + 1) * half], odd[tap * half : (tap + 1) * half]
                top, low = tap * taps, tap * taps + half
                wp[layer, p, top : top + half, :] = jnp.concatenate(
                    [e[:, :half], zero, e[:, half:], zero], axis=1
                )
                wp[layer, p, low : low + half, :] = jnp.concatenate(
                    [zero, o[:, :half], zero, o[:, half:]], axis=1
                )
            be, bo = bv[layer, 2 * p : 2 * p + 1], bv[layer, 2 * p + 1 : 2 * p + 2]
            at_row = layer * pairs + p
            bp[at_row : at_row + 1, :] = jnp.concatenate(
                [be[:, :half], bo[:, :half], be[:, half:], bo[:, half:]], axis=1
            )

    def gated(slot, layer, earlier, current):
        for p in range(pairs):
            cols = slice(p * taps, (p + 1) * taps)
            z = jnp.dot(
                jnp.concatenate([earlier[:, cols], current[:, cols]], axis=1),
                wp[layer, p],
                preferred_element_type=jnp.float32,
            )
            row = layer * pairs + p
            z = z + bp[row : row + 1, :]
            h = jnp.tanh(z[:, :taps]) * (0.5 * jnp.tanh(0.5 * z[:, taps:]) + 0.5)
            hid[block(slot), cols] = h.astype(jnp.bfloat16)
        hid_copy(slot).start()

    def mixed(slot, layer, current):
        mine = mv[layer, pl.ds(pl.multiple_of(c * width, width), width), :]
        theirs = mv[layer, pl.ds(pl.multiple_of((1 - c) * width, width), width), :]
        acc = jnp.dot(hid[block(slot)], mine, preferred_element_type=jnp.float32)
        hid_copy(slot).wait_recv()
        acc = acc + jnp.dot(oth[block(slot)], theirs, preferred_element_type=jnp.float32)
        return (current.astype(jnp.float32) + acc).astype(jnp.bfloat16)

    def first_gated(buf, k, slot):
        window = buf[block(k, size=rows + EDGE)]
        shifted = pltpu.roll(window.astype(jnp.float32), 1, 0)[EDGE:].astype(jnp.bfloat16)
        gated(slot, 0, shifted, window[EDGE:])

    def own_finish(k):
        x1[block(k)] = mixed(k, 0, xbuf[block(k, EDGE)])

        @pl.when(jnp.logical_and(sends, k >= raw_chunks))
        def _():
            x1_copy(k).start()

    loads[0].wait()
    loads[1].wait()
    pack_weights(0)

    @pl.when(jnp.logical_not(has_prev))
    def _():
        xbuf[:EDGE] = jnp.zeros((EDGE, width), jnp.bfloat16)

    @pl.when(jnp.logical_not(receives))
    def _():
        far[...] = jnp.zeros((total, width), jnp.bfloat16)

    pl.when(has_prev)(edge_copy.wait_recv)
    pl.when(sends)(raw_edge_copy.start)
    first_gated(xbuf, 0, 0)
    loads[3].wait()

    @pl.loop(1, chunks)
    def _(k):
        first_gated(xbuf, k, k)
        own_finish(k - 1)

    own_finish(chunks - 1)

    pack_weights(1)
    loads[4].wait()

    @pl.when(receives)
    def _():
        raw_copy.wait_recv()
        raw_edge_copy.wait_recv()

        @pl.loop(0, raw_chunks)
        def _(k):
            first_gated(raw, k, chunks + k)
            far[block(k)] = mixed(chunks + k, 0, raw[block(k, EDGE)])

    @pl.loop(0, chunks)
    def _(k):
        @pl.when(jnp.logical_and(receives, k >= raw_chunks))
        def _():
            x1_copy(k).wait_recv()

        slot = chunks + raw_chunks + k
        current = x1[block(k)]
        gated(slot, 1, far[block(k)], current)
        obuf[block(k)] = mixed(slot, 1, current)
        out_copy(k).start()

    @pl.loop(0, chunks)
    def _(k):
        out_copy(k).wait()
        hid_copy(k).wait_send()
        hid_copy(chunks + raw_chunks + k).wait_send()

        @pl.when(jnp.logical_and(sends, k >= raw_chunks))
        def _():
            x1_copy(k).wait_send()

    @pl.when(receives)
    def _():
        @pl.loop(0, raw_chunks)
        def _(k):
            hid_copy(chunks + k).wait_send()

    pl.when(has_next)(edge_copy.wait_send)

    @pl.when(sends)
    def _():
        raw_copy.wait_send()
        raw_edge_copy.wait_send()


def shards(length, signal, kernel_weight_stack, conv_bias, mix_weight):
    total, width = signal.shape
    layers, groups, taps, _ = kernel_weight_stack.shape
    reach = SECOND_DILATION // total
    rows, raw_rows = 128, 128
    chunks = total // rows
    slots = 2 * chunks + raw_rows // rows
    bf16, f32 = jnp.bfloat16, jnp.float32
    dma = pltpu.SemaphoreType.DMA
    return pl.pallas_call(
        functools.partial(layers_kernel, length, reach, rows, raw_rows),
        out_shape=jax.ShapeDtypeStruct(signal.shape, bf16),
        in_specs=[pl.BlockSpec(memory_space=pltpu.HBM)] * 4,
        out_specs=pl.BlockSpec(memory_space=pl.ANY),
        scratch_shapes=[
            pltpu.VMEM((EDGE + total, width), bf16),
            pltpu.VMEM((EDGE + raw_rows, width), bf16),
            pltpu.VMEM((total, width), bf16),
            pltpu.VMEM((total, width), bf16),
            pltpu.VMEM((slots * rows, width), bf16),
            pltpu.VMEM((slots * rows, width), bf16),
            pltpu.VMEM(kernel_weight_stack.shape, bf16),
            pltpu.VMEM((layers, groups // 2, 2 * taps, 2 * taps), bf16),
            pltpu.VMEM(conv_bias.shape, f32),
            pltpu.VMEM((layers * groups // 2, 2 * taps), f32),
            pltpu.VMEM(mix_weight.shape, bf16),
            pltpu.VMEM((total, width), bf16),
            dma((6,)),
            dma((2,)),
            dma((2,)),
            dma((2,)),
            dma((chunks,)),
            dma((chunks,)),
            dma((slots,)),
            dma((slots,)),
            dma((chunks,)),
        ],
        compiler_params=pltpu.CompilerParams(
            collective_id=0, has_side_effects=True, vmem_limit_bytes=40 << 20
        ),
    )(*(pltpu.with_memory_space_constraint(a, pltpu.HBM) for a in (signal, kernel_weight_stack, conv_bias, mix_weight)))


def solution(mesh):
    placed = (
        P(("parts", "tm"), "chan"),
        P(None, "chan", None, None),
        P(None, "chan", None),
        P(None, None, "chan"),
    )
    return jax.shard_map(
        functools.partial(shards, mesh.shape["tm"]),
        mesh=mesh,
        in_specs=placed,
        out_specs=P(("parts", "tm"), "chan"),
        check_vma=False,
    )
```

```python
import functools

import jax
import jax.numpy as jnp
from jax import lax
from jax.experimental import pallas as pl
from jax.experimental.pallas import tpu as pltpu
from jax.sharding import PartitionSpec as P

SECOND_DILATION = 4096
EDGE = 16
MESH = pl.DeviceIdType.MESH


def layers_kernel(
    length, reach, rows, raw_rows,
    sig, kws, bias, mix, out,
    xbuf, raw, far, x1, hid, oth, kv, wp, bv, bp, mv, obuf, tail,
    load_sem, edge_sem, raw_sem, fwd_sem, x1_send, x1_recv, hid_send, hid_recv, out_sem,
):
    total, width = sig.shape
    groups, taps = kws.shape[1], kws.shape[2]
    half = taps // 2
    pairs = groups // 2
    chunks, raw_chunks = total // rows, raw_rows // rows
    part, t, c = lax.axis_index("parts"), lax.axis_index("tm"), lax.axis_index("chan")
    has_next, has_prev = t < length - 1, t > 0
    sends, receives = t < length - reach, t >= reach

    def at(step):
        return (part, lax.rem(t + step + length, length), c)

    peer = (part, t, 1 - c)

    barrier = pltpu.get_barrier_semaphore()
    for there, step in ((has_next, 1), (has_prev, -1), (sends, reach), (receives, -reach)):

        @pl.when(there)
        def _(step=step):
            pl.semaphore_signal(barrier, inc=1, device_id=at(step), device_id_type=MESH)

    pl.semaphore_signal(barrier, inc=1, device_id=peer, device_id_type=MESH)

    loads = [
        pltpu.make_async_copy(src, dst, load_sem.at[i])
        for i, (src, dst) in enumerate(
            (
                (kws, kv),
                (bias, bv),
                (sig.at[pl.ds(raw_rows, total - raw_rows)], xbuf.at[pl.ds(EDGE + raw_rows, total - raw_rows)]),
                (mix.at[0], mv.at[0]),
                (mix.at[1], mv.at[1]),
            )
        )
    ]
    head_copy = pltpu.make_async_copy(
        sig.at[pl.ds(0, raw_rows)], xbuf.at[pl.ds(EDGE, raw_rows)], load_sem.at[5]
    )
    tail_copy = pltpu.make_async_copy(sig.at[pl.ds(total - EDGE, EDGE)], tail, load_sem.at[6])
    tail_copy.start()
    head_copy.start()
    for i in (2, 0, 1, 3, 4):
        loads[i].start()

    partners = 1
    for there in (has_next, has_prev, sends, receives):
        partners = partners + there.astype(jnp.int32)
    pl.semaphore_wait(barrier, partners)

    def remote(src, dst, send, recv, to):
        return pltpu.make_async_remote_copy(
            src_ref=src, dst_ref=dst, send_sem=send, recv_sem=recv, device_id=to, device_id_type=MESH
        )

    edge_copy = remote(
        tail, xbuf.at[pl.ds(0, EDGE)], edge_sem.at[0], edge_sem.at[1], at(1)
    )
    raw_copy = remote(
        xbuf.at[pl.ds(EDGE, raw_rows)], raw.at[pl.ds(EDGE, raw_rows)], raw_sem.at[0], raw_sem.at[1], at(reach)
    )
    raw_edge_copy = remote(
        xbuf.at[pl.ds(0, EDGE)], raw.at[pl.ds(0, EDGE)], fwd_sem.at[0], fwd_sem.at[1], at(reach)
    )
    tail_copy.wait()
    pl.when(has_next)(edge_copy.start)
    head_copy.wait()
    pl.when(sends)(raw_copy.start)

    def block(k, offset=0, size=rows):
        return pl.ds(pl.multiple_of(k * rows + offset, EDGE), size)

    def x1_copy(k):
        return remote(x1.at[block(k)], far.at[block(k)], x1_send.at[k], x1_recv.at[k], at(reach))

    def hid_copy(k):
        return remote(hid.at[block(k)], oth.at[block(k)], hid_send.at[k], hid_recv.at[k], peer)

    def out_copy(k):
        return pltpu.make_async_copy(obuf.at[block(k)], out.at[block(k)], out_sem.at[k])

    def pack_weights(layer):
        zero = jnp.zeros((half, half), jnp.bfloat16)
        for p in range(pairs):
            even, odd = kv[layer, 2 * p], kv[layer, 2 * p + 1]
            for tap in range(2):
                e, o = even[tap * half : (tap + 1) * half], odd[tap * half : (tap + 1) * half]
                top, low = tap * taps, tap * taps + half
                wp[layer, p, top : top + half, :] = jnp.concatenate(
                    [e[:, :half], zero, e[:, half:], zero], axis=1
                )
                wp[layer, p, low : low + half, :] = jnp.concatenate(
                    [zero, o[:, :half], zero, o[:, half:]], axis=1
                )
            be, bo = bv[layer, 2 * p : 2 * p + 1], bv[layer, 2 * p + 1 : 2 * p + 2]
            at_row = layer * pairs + p
            bp[at_row : at_row + 1, :] = jnp.concatenate(
                [be[:, :half], bo[:, :half], be[:, half:], bo[:, half:]], axis=1
            )

    def gated(slot, layer, earlier, current):
        for p in range(pairs):
            cols = slice(p * taps, (p + 1) * taps)
            z = jnp.dot(
                jnp.concatenate([earlier[:, cols], current[:, cols]], axis=1),
                wp[layer, p],
                preferred_element_type=jnp.float32,
            )
            row = layer * pairs + p
            z = z + bp[row : row + 1, :]
            h = jnp.tanh(z[:, :taps]) * (0.5 * jnp.tanh(0.5 * z[:, taps:]) + 0.5)
            hid[block(slot), cols] = h.astype(jnp.bfloat16)
        hid_copy(slot).start()

    def mixed(slot, layer, current):
        mine = mv[layer, pl.ds(pl.multiple_of(c * width, width), width), :]
        theirs = mv[layer, pl.ds(pl.multiple_of((1 - c) * width, width), width), :]
        acc = jnp.dot(hid[block(slot)], mine, preferred_element_type=jnp.float32)
        hid_copy(slot).wait_recv()
        acc = acc + jnp.dot(oth[block(slot)], theirs, preferred_element_type=jnp.float32)
        return (current.astype(jnp.float32) + acc).astype(jnp.bfloat16)

    def first_gated(buf, k, slot):
        window = buf[block(k, size=rows + EDGE)]
        shifted = pltpu.roll(window.astype(jnp.float32), 1, 0)[EDGE:].astype(jnp.bfloat16)
        gated(slot, 0, shifted, window[EDGE:])

    def own_finish(k):
        x1[block(k)] = mixed(k, 0, xbuf[block(k, EDGE)])

        @pl.when(jnp.logical_and(sends, k >= raw_chunks))
        def _():
            x1_copy(k).start()

    loads[0].wait()
    loads[1].wait()
    pack_weights(0)

    @pl.when(jnp.logical_not(has_prev))
    def _():
        xbuf[:EDGE] = jnp.zeros((EDGE, width), jnp.bfloat16)

    @pl.when(jnp.logical_not(receives))
    def _():
        far[...] = jnp.zeros((total, width), jnp.bfloat16)

    pl.when(has_prev)(edge_copy.wait_recv)
    pl.when(sends)(raw_edge_copy.start)
    loads[2].wait()
    first_gated(xbuf, 0, 0)
    loads[3].wait()

    @pl.loop(1, chunks)
    def _(k):
        first_gated(xbuf, k, k)
        own_finish(k - 1)

    own_finish(chunks - 1)

    pack_weights(1)
    loads[4].wait()

    @pl.when(receives)
    def _():
        raw_copy.wait_recv()
        raw_edge_copy.wait_recv()

        @pl.loop(0, raw_chunks)
        def _(k):
            first_gated(raw, k, chunks + k)
            far[block(k)] = mixed(chunks + k, 0, raw[block(k, EDGE)])

    @pl.loop(0, chunks)
    def _(k):
        @pl.when(jnp.logical_and(receives, k >= raw_chunks))
        def _():
            x1_copy(k).wait_recv()

        slot = chunks + raw_chunks + k
        current = x1[block(k)]
        gated(slot, 1, far[block(k)], current)
        obuf[block(k)] = mixed(slot, 1, current)
        out_copy(k).start()

    @pl.loop(0, chunks)
    def _(k):
        out_copy(k).wait()
        hid_copy(k).wait_send()
        hid_copy(chunks + raw_chunks + k).wait_send()

        @pl.when(jnp.logical_and(sends, k >= raw_chunks))
        def _():
            x1_copy(k).wait_send()

    @pl.when(receives)
    def _():
        @pl.loop(0, raw_chunks)
        def _(k):
            hid_copy(chunks + k).wait_send()

    pl.when(has_next)(edge_copy.wait_send)

    @pl.when(sends)
    def _():
        raw_copy.wait_send()
        raw_edge_copy.wait_send()


def shards(length, signal, kernel_weight_stack, conv_bias, mix_weight):
    total, width = signal.shape
    layers, groups, taps, _ = kernel_weight_stack.shape
    reach = SECOND_DILATION // total
    rows, raw_rows = 128, 128
    chunks = total // rows
    slots = 2 * chunks + raw_rows // rows
    bf16, f32 = jnp.bfloat16, jnp.float32
    dma = pltpu.SemaphoreType.DMA
    return pl.pallas_call(
        functools.partial(layers_kernel, length, reach, rows, raw_rows),
        out_shape=jax.ShapeDtypeStruct(signal.shape, bf16),
        in_specs=[pl.BlockSpec(memory_space=pltpu.HBM)] * 4,
        out_specs=pl.BlockSpec(memory_space=pl.ANY),
        scratch_shapes=[
            pltpu.VMEM((EDGE + total, width), bf16),
            pltpu.VMEM((EDGE + raw_rows, width), bf16),
            pltpu.VMEM((total, width), bf16),
            pltpu.VMEM((total, width), bf16),
            pltpu.VMEM((slots * rows, width), bf16),
            pltpu.VMEM((slots * rows, width), bf16),
            pltpu.VMEM(kernel_weight_stack.shape, bf16),
            pltpu.VMEM((layers, groups // 2, 2 * taps, 2 * taps), bf16),
            pltpu.VMEM(conv_bias.shape, f32),
            pltpu.VMEM((layers * groups // 2, 2 * taps), f32),
            pltpu.VMEM(mix_weight.shape, bf16),
            pltpu.VMEM((total, width), bf16),
            pltpu.VMEM((EDGE, width), bf16),
            dma((7,)),
            dma((2,)),
            dma((2,)),
            dma((2,)),
            dma((chunks,)),
            dma((chunks,)),
            dma((slots,)),
            dma((slots,)),
            dma((chunks,)),
        ],
        compiler_params=pltpu.CompilerParams(
            collective_id=0, has_side_effects=True, vmem_limit_bytes=40 << 20
        ),
    )(*(pltpu.with_memory_space_constraint(a, pltpu.HBM) for a in (signal, kernel_weight_stack, conv_bias, mix_weight)))


def solution(mesh):
    placed = (
        P(("parts", "tm"), "chan"),
        P(None, "chan", None, None),
        P(None, "chan", None),
        P(None, None, "chan"),
    )
    return jax.shard_map(
        functools.partial(shards, mesh.shape["tm"]),
        mesh=mesh,
        in_specs=placed,
        out_specs=P(("parts", "tm"), "chan"),
        check_vma=False,
    )
```

```python
import functools

import jax
import jax.numpy as jnp
from jax import lax
from jax.experimental import pallas as pl
from jax.experimental.pallas import tpu as pltpu
from jax.sharding import PartitionSpec as P

SECOND_DILATION = 4096
EDGE = 16
MESH = pl.DeviceIdType.MESH


def layers_kernel(
    length, reach, rows, raw_rows,
    sig, kws, bias, mix, out,
    xbuf, raw, far, x1, hid, oth, kv, wp, bv, bp, mv, obuf, tail, packed, got,
    load_sem, edge_sem, raw_sem, fwd_sem, x1_send, x1_recv, hid_send, hid_recv, out_sem,
):
    total, width = sig.shape
    groups, taps = kws.shape[1], kws.shape[2]
    half = taps // 2
    pairs = groups // 2
    chunks, raw_chunks = total // rows, raw_rows // rows
    part, t, c = lax.axis_index("parts"), lax.axis_index("tm"), lax.axis_index("chan")
    has_next, has_prev = t < length - 1, t > 0
    sends, receives = t < length - reach, t >= reach

    def at(step):
        return (part, lax.rem(t + step + length, length), c)

    peer = (part, t, 1 - c)

    barrier = pltpu.get_barrier_semaphore()
    for there, step in ((has_next, 1), (has_prev, -1), (sends, reach), (receives, -reach)):

        @pl.when(there)
        def _(step=step):
            pl.semaphore_signal(barrier, inc=1, device_id=at(step), device_id_type=MESH)

    pl.semaphore_signal(barrier, inc=1, device_id=peer, device_id_type=MESH)

    loads = [
        pltpu.make_async_copy(src, dst, load_sem.at[i])
        for i, (src, dst) in enumerate(
            (
                (kws, kv),
                (bias, bv),
                (sig.at[pl.ds(raw_rows, total - raw_rows)], xbuf.at[pl.ds(EDGE + raw_rows, total - raw_rows)]),
                (mix.at[0], mv.at[0]),
                (mix.at[1], mv.at[1]),
            )
        )
    ]
    head_copy = pltpu.make_async_copy(
        sig.at[pl.ds(0, raw_rows)], xbuf.at[pl.ds(EDGE, raw_rows)], load_sem.at[5]
    )
    tail_copy = pltpu.make_async_copy(sig.at[pl.ds(total - EDGE, EDGE)], tail, load_sem.at[6])
    tail_copy.start()
    head_copy.start()
    for i in (2, 0, 1, 3, 4):
        loads[i].start()

    partners = 1
    for there in (has_next, has_prev, sends, receives):
        partners = partners + there.astype(jnp.int32)
    pl.semaphore_wait(barrier, partners)

    def remote(src, dst, send, recv, to):
        return pltpu.make_async_remote_copy(
            src_ref=src, dst_ref=dst, send_sem=send, recv_sem=recv, device_id=to, device_id_type=MESH
        )

    edge_copy = remote(
        tail, xbuf.at[pl.ds(0, EDGE)], edge_sem.at[0], edge_sem.at[1], at(1)
    )
    raw_copy = remote(
        xbuf.at[pl.ds(EDGE, raw_rows)], raw.at[pl.ds(EDGE, raw_rows)], raw_sem.at[0], raw_sem.at[1], at(reach)
    )
    raw_edge_copy = remote(
        packed, got, fwd_sem.at[0], fwd_sem.at[1], at(reach)
    )
    tail_copy.wait()
    pl.when(has_next)(edge_copy.start)
    head_copy.wait()
    pl.when(sends)(raw_copy.start)

    def block(k, offset=0, size=rows):
        return pl.ds(pl.multiple_of(k * rows + offset, EDGE), size)

    def x1_copy(k):
        return remote(x1.at[block(k)], far.at[block(k)], x1_send.at[k], x1_recv.at[k], at(reach))

    def hid_copy(k):
        return remote(hid.at[block(k)], oth.at[block(k)], hid_send.at[k], hid_recv.at[k], peer)

    def out_copy(k):
        return pltpu.make_async_copy(obuf.at[block(k)], out.at[block(k)], out_sem.at[k])

    def pack_weights(layer):
        zero = jnp.zeros((half, half), jnp.bfloat16)
        for p in range(pairs):
            even, odd = kv[layer, 2 * p], kv[layer, 2 * p + 1]
            for tap in range(2):
                e, o = even[tap * half : (tap + 1) * half], odd[tap * half : (tap + 1) * half]
                top, low = tap * taps, tap * taps + half
                wp[layer, p, top : top + half, :] = jnp.concatenate(
                    [e[:, :half], zero, e[:, half:], zero], axis=1
                )
                wp[layer, p, low : low + half, :] = jnp.concatenate(
                    [zero, o[:, :half], zero, o[:, half:]], axis=1
                )
            be, bo = bv[layer, 2 * p : 2 * p + 1], bv[layer, 2 * p + 1 : 2 * p + 2]
            at_row = layer * pairs + p
            bp[at_row : at_row + 1, :] = jnp.concatenate(
                [be[:, :half], bo[:, :half], be[:, half:], bo[:, half:]], axis=1
            )

    def gated(slot, layer, earlier, current):
        for p in range(pairs):
            cols = slice(p * taps, (p + 1) * taps)
            z = jnp.dot(
                jnp.concatenate([earlier[:, cols], current[:, cols]], axis=1),
                wp[layer, p],
                preferred_element_type=jnp.float32,
            )
            row = layer * pairs + p
            z = z + bp[row : row + 1, :]
            h = jnp.tanh(z[:, :taps]) * (0.5 * jnp.tanh(0.5 * z[:, taps:]) + 0.5)
            hid[block(slot), cols] = h.astype(jnp.bfloat16)
        hid_copy(slot).start()

    def mixed(slot, layer, current):
        mine = mv[layer, pl.ds(pl.multiple_of(c * width, width), width), :]
        theirs = mv[layer, pl.ds(pl.multiple_of((1 - c) * width, width), width), :]
        acc = jnp.dot(hid[block(slot)], mine, preferred_element_type=jnp.float32)
        hid_copy(slot).wait_recv()
        acc = acc + jnp.dot(oth[block(slot)], theirs, preferred_element_type=jnp.float32)
        return (current.astype(jnp.float32) + acc).astype(jnp.bfloat16)

    def first_gated(buf, k, slot):
        window = buf[block(k, size=rows + EDGE)]
        shifted = pltpu.roll(window.astype(jnp.float32), 1, 0)[EDGE:].astype(jnp.bfloat16)
        gated(slot, 0, shifted, window[EDGE:])

    def own_finish(k):
        x1[block(k)] = mixed(k, 0, xbuf[block(k, EDGE)])

        @pl.when(jnp.logical_and(sends, k >= raw_chunks))
        def _():
            x1_copy(k).start()

    loads[0].wait()
    loads[1].wait()
    pack_weights(0)

    @pl.when(jnp.logical_not(has_prev))
    def _():
        xbuf[:EDGE] = jnp.zeros((EDGE, width), jnp.bfloat16)

    @pl.when(jnp.logical_not(receives))
    def _():
        far[...] = jnp.zeros((total, width), jnp.bfloat16)

    pl.when(has_prev)(edge_copy.wait_recv)
    last = xbuf[:EDGE].astype(jnp.float32)[EDGE - 1 :]
    at_row = lax.broadcasted_iota(jnp.int32, (EDGE, 128), 0)
    tile = jnp.zeros((EDGE, 128), jnp.float32)
    for j in range(width // 128):
        tile = jnp.where(at_row == j, last[:, j * 128 : (j + 1) * 128], tile)
    packed[...] = tile.astype(jnp.bfloat16)
    pl.when(sends)(raw_edge_copy.start)
    loads[2].wait()
    first_gated(xbuf, 0, 0)
    loads[3].wait()

    @pl.loop(1, chunks)
    def _(k):
        first_gated(xbuf, k, k)
        own_finish(k - 1)

    own_finish(chunks - 1)

    pack_weights(1)
    loads[4].wait()

    @pl.when(receives)
    def _():
        raw_copy.wait_recv()
        raw_edge_copy.wait_recv()
        tile = got[...].astype(jnp.float32)
        for j in range(width // 128):
            row = jnp.broadcast_to(tile[j : j + 1], (EDGE, 128))
            raw[:EDGE, j * 128 : (j + 1) * 128] = row.astype(jnp.bfloat16)

        @pl.loop(0, raw_chunks)
        def _(k):
            first_gated(raw, k, chunks + k)
            far[block(k)] = mixed(chunks + k, 0, raw[block(k, EDGE)])

    @pl.loop(0, chunks)
    def _(k):
        @pl.when(jnp.logical_and(receives, k >= raw_chunks))
        def _():
            x1_copy(k).wait_recv()

        slot = chunks + raw_chunks + k
        current = x1[block(k)]
        gated(slot, 1, far[block(k)], current)
        obuf[block(k)] = mixed(slot, 1, current)
        out_copy(k).start()

    @pl.loop(0, chunks)
    def _(k):
        out_copy(k).wait()
        hid_copy(k).wait_send()
        hid_copy(chunks + raw_chunks + k).wait_send()

        @pl.when(jnp.logical_and(sends, k >= raw_chunks))
        def _():
            x1_copy(k).wait_send()

    @pl.when(receives)
    def _():
        @pl.loop(0, raw_chunks)
        def _(k):
            hid_copy(chunks + k).wait_send()

    pl.when(has_next)(edge_copy.wait_send)

    @pl.when(sends)
    def _():
        raw_copy.wait_send()
        raw_edge_copy.wait_send()


def shards(length, signal, kernel_weight_stack, conv_bias, mix_weight):
    total, width = signal.shape
    layers, groups, taps, _ = kernel_weight_stack.shape
    reach = SECOND_DILATION // total
    rows, raw_rows = 128, 128
    chunks = total // rows
    slots = 2 * chunks + raw_rows // rows
    bf16, f32 = jnp.bfloat16, jnp.float32
    dma = pltpu.SemaphoreType.DMA
    return pl.pallas_call(
        functools.partial(layers_kernel, length, reach, rows, raw_rows),
        out_shape=jax.ShapeDtypeStruct(signal.shape, bf16),
        in_specs=[pl.BlockSpec(memory_space=pltpu.HBM)] * 4,
        out_specs=pl.BlockSpec(memory_space=pl.ANY),
        scratch_shapes=[
            pltpu.VMEM((EDGE + total, width), bf16),
            pltpu.VMEM((EDGE + raw_rows, width), bf16),
            pltpu.VMEM((total, width), bf16),
            pltpu.VMEM((total, width), bf16),
            pltpu.VMEM((slots * rows, width), bf16),
            pltpu.VMEM((slots * rows, width), bf16),
            pltpu.VMEM(kernel_weight_stack.shape, bf16),
            pltpu.VMEM((layers, groups // 2, 2 * taps, 2 * taps), bf16),
            pltpu.VMEM(conv_bias.shape, f32),
            pltpu.VMEM((layers * groups // 2, 2 * taps), f32),
            pltpu.VMEM(mix_weight.shape, bf16),
            pltpu.VMEM((total, width), bf16),
            pltpu.VMEM((EDGE, width), bf16),
            pltpu.VMEM((EDGE, 128), bf16),
            pltpu.VMEM((EDGE, 128), bf16),
            dma((7,)),
            dma((2,)),
            dma((2,)),
            dma((2,)),
            dma((chunks,)),
            dma((chunks,)),
            dma((slots,)),
            dma((slots,)),
            dma((chunks,)),
        ],
        compiler_params=pltpu.CompilerParams(
            collective_id=0, has_side_effects=True, vmem_limit_bytes=40 << 20
        ),
    )(*(pltpu.with_memory_space_constraint(a, pltpu.HBM) for a in (signal, kernel_weight_stack, conv_bias, mix_weight)))


def solution(mesh):
    placed = (
        P(("parts", "tm"), "chan"),
        P(None, "chan", None, None),
        P(None, "chan", None),
        P(None, None, "chan"),
    )
    return jax.shard_map(
        functools.partial(shards, mesh.shape["tm"]),
        mesh=mesh,
        in_specs=placed,
        out_specs=P(("parts", "tm"), "chan"),
        check_vma=False,
    )
```
